256 devices in a mesh: tm: 8 (over z), panel: 32 (over y, x, core).
Axes of the slice: x: 4, y: 4, z: 8, core: 2. Of those that a mesh axis runs over, the one named last changes fastest.
Arguments:
- boundary: float32 [8, 2048, 2048], P('tm', 'panel'), may hold values from -6 to 6
- far_coupling: float32 [8, 2048, 2048], P('tm', 'panel'), may hold values from -6 to 6
- cross_coupling: float32 [8, 2048, 2048], P('tm', 'panel'), may hold values from -6 to 6
- tail_coupling: float32 [8, 2048, 2048], P('tm', 'panel'), may hold values from -6 to 6
- arrow_block: float32 [8, 2048, 64], P('tm', 'panel'), may hold values from -0.125 to 0.125
- inverse_map: bfloat16 [8, 3, 2048, 2048], P('tm', None, 'panel'), may hold values from -0.03125 to 0.03125
- fill_map: bfloat16 [8, 3, 2048, 2048], P('tm', None, 'panel'), may hold values from -0.03125 to 0.03125
- cross_map: bfloat16 [8, 3, 2048, 2048], P('tm', None, 'panel'), may hold values from -0.03125 to 0.03125
- tail_map: bfloat16 [8, 3, 2048, 2048], P('tm', None, 'panel'), may hold values from -0.03125 to 0.03125
- arrow_tip: float32 [64, 64], replicated, may hold values from -6 to 6
- inverse_diagonal: float32 [8, 2048], P('tm', 'panel'), may hold values from 0.05 to 20
Outputs:
- schur_block: float32 [8, 2048, 2048], P('tm', 'panel')
- far_fill: float32 [8, 2048, 2048], P('tm', 'panel')
- cross_fill: float32 [8, 2048, 2048], P('tm', 'panel')
- tail_fill: float32 [8, 2048, 2048], P('tm', 'panel')
- arrow_cols: float32 [8, 2048, 64], P('tm', 'panel')
- tip_schur: float32 [64, 64], replicated
The draws below stay inside these ranges and needn't reach their ends.
All inputs are finite; a program needn't handle non-finite values.
Results may differ from the reference program's by a relative error of at most 0.0013.
Values may be sent and summed in bfloat16 or wider, within the bound.
No kernel may reach another device: no remote copies, remote signals or barrier semaphores. Data moves between devices by JAX's collectives and lax.ppermute only.
A program may use at most 128 MiB of HBM per device.

```python
import math
import jax
import jax.numpy as jnp
import numpy as np
from jax import lax

BLOCK = 2048
ARROW = 64
LEVELS = 3
N_TM = 8


def block_levels(stream_key, extent, cuts, least, largest):
    def one(dim, blocks):
        heights = jax.random.uniform(jax.random.fold_in(jax.random.fold_in(stream_key, 6), dim), (blocks,), jnp.float32, least / len(cuts), largest / len(cuts))
        return jnp.repeat(jnp.exp(heights), extent[dim] // blocks).reshape((-1,) + (1,) * (len(extent) - dim - 1))

    factor_of = one(*cuts[0])
    for cut in cuts[1:]:
        factor_of = factor_of * one(*cut)
    return factor_of


def normal_values(rng, extent, width, bound, split=(), held_as=jnp.bfloat16):
    entries = jax.random.normal(rng, extent, jnp.float32) * width
    if len(split) > 0:
        entries = block_levels(rng, extent, split, -0.22, 0.18) * entries
    return jnp.clip(entries, min=-bound, max=bound).astype(held_as)


def setup_inputs(seed: int = 0) -> dict:
    keys = jax.random.split(jax.random.key(seed), 12)
    boundary = normal_values(keys[0], (N_TM, BLOCK, BLOCK), 1.0, 6.0, ((0, 8), (1, 32)), jnp.float32)
    far_coupling = normal_values(keys[1], (N_TM, BLOCK, BLOCK), 1.0, 6.0, ((0, 8), (1, 32)), jnp.float32)
    cross_coupling = normal_values(keys[2], (N_TM, BLOCK, BLOCK), 1.0, 6.0, ((0, 8), (1, 32)), jnp.float32)
    tail_coupling = normal_values(keys[3], (N_TM, BLOCK, BLOCK), 1.0, 6.0, ((0, 8), (1, 32)), jnp.float32)
    arrow_block = normal_values(keys[4], (N_TM, BLOCK, ARROW), ((BLOCK * N_TM) ** -0.5), 0.125, ((0, 8), (1, 32)), jnp.float32)
    inverse_map = normal_values(keys[5], (N_TM, LEVELS, BLOCK, BLOCK), (16 * BLOCK) ** -0.5, 0.03125, ((0, 8), (2, 32)))
    fill_map = normal_values(keys[6], (N_TM, LEVELS, BLOCK, BLOCK), (16 * BLOCK) ** -0.5, 0.03125, ((0, 8), (2, 32)))
    cross_map = normal_values(keys[7], (N_TM, LEVELS, BLOCK, BLOCK), (16 * BLOCK) ** -0.5, 0.03125, ((0, 8), (2, 32)))
    tail_map = normal_values(keys[8], (N_TM, LEVELS, BLOCK, BLOCK), (16 * BLOCK) ** -0.5, 0.03125, ((0, 8), (2, 32)))
    arrow_tip = normal_values(keys[9], (ARROW, ARROW), 1.0, 6.0, (), jnp.float32)
    inverse_diagonal = jnp.clip(jnp.exp(math.log(20.0) - 5.9914645 * jax.random.uniform(keys[10], (N_TM, BLOCK), jnp.float32) ** block_levels(keys[10], (N_TM, BLOCK), ((0, 8), (1, 32)), -0.2, 0.2)), 0.05, 20.0)
    return {"boundary": boundary, "far_coupling": far_coupling, "cross_coupling": cross_coupling, "tail_coupling": tail_coupling, "arrow_block": arrow_block, "inverse_map": inverse_map, "fill_map": fill_map, "cross_map": cross_map, "tail_map": tail_map, "arrow_tip": arrow_tip, "inverse_diagonal": inverse_diagonal}


def multiply(operands):
    return jnp.dot(operands[0], operands[1], preferred_element_type=jnp.float32)


def reference(boundary, far_coupling, cross_coupling, tail_coupling, arrow_block, inverse_map, fill_map, cross_map, tail_map, arrow_tip, inverse_diagonal):
    schur_block = boundary.astype(jnp.float32)
    far_fill = far_coupling.astype(jnp.float32)
    cross_fill = cross_coupling.astype(jnp.float32)
    tail_fill = tail_coupling.astype(jnp.float32)
    arrow_cols = arrow_block.astype(jnp.float32)
    block_rows = schur_block.shape[1]
    for merge_level in range(LEVELS):
        partner = np.arange(N_TM) ^ (1 << merge_level)
        outgoing = jnp.concatenate([schur_block, arrow_cols], axis=2).astype(jnp.bfloat16)
        received = outgoing[partner]
        level_maps = jnp.concatenate([inverse_map[:, merge_level], fill_map[:, merge_level], cross_map[:, merge_level], tail_map[:, merge_level]], axis=1)
        update = lax.map(multiply, (level_maps, received))
        schur_block = schur_block - update[:, :block_rows, :block_rows]
        far_fill = far_fill - update[:, block_rows:2 * block_rows, :block_rows]
        cross_fill = cross_fill - update[:, 2 * block_rows:3 * block_rows, :block_rows]
        tail_fill = tail_fill - update[:, 3 * block_rows:, :block_rows]
        arrow_cols = arrow_cols - update[:, :block_rows, block_rows:]
    weighted = arrow_cols * inverse_diagonal[:, :, None]
    tip_schur = arrow_tip - jnp.einsum("pkb,pkc->bc", weighted, arrow_cols, precision=lax.Precision.HIGHEST)
    return schur_block, far_fill, cross_fill, tail_fill, arrow_cols, tip_schur
```

```python
import functools

import jax
import jax.numpy as jnp
from jax import lax
from jax.experimental import pallas as pl
from jax.experimental.pallas import tpu as pltpu
from jax.sharding import PartitionSpec as P

F32 = jnp.float32
BF16 = jnp.bfloat16
SIDE = 4
CHIPS = SIDE * SIDE
TILE = 256
ANY = pl.BlockSpec(memory_space=pl.ANY)
VMEM = pl.BlockSpec(memory_space=pltpu.VMEM)
SMEM = pl.BlockSpec(memory_space=pltpu.SMEM)
NT = (((1,), (1,)), ((), ()))


def panel_index(y, x, core):
    return (y * SIDE + x) * 2 + core


def ring(first, step):
    route = []
    for y in range(SIDE):
        for x in range(SIDE):
            for core in range(2):
                if core == first:
                    to = panel_index(y, (x + step) % SIDE, core)
                else:
                    to = panel_index((y + step) % SIDE, x, core)
                route.append((panel_index(y, x, core), to))
    return route


SWAP = [(i, i ^ 1) for i in range(2 * CHIPS)]
XOR_X = {k: [(panel_index(y, x, c), panel_index(y, x ^ k, c)) for y in range(SIDE) for x in range(SIDE) for c in range(2)] for k in (1, 2, 3)}
XOR_Y = {k: [(panel_index(y, x, c), panel_index(y ^ k, x, c)) for y in range(SIDE) for x in range(SIDE) for c in range(2)] for k in (1, 2, 3)}


def flip(block, bit):
    count = lax.axis_size("tm")
    return lax.ppermute(block, "tm", [(p, p ^ bit) for p in range(count)])


def params(**kw):
    return pltpu.CompilerParams(vmem_limit_bytes=24 * 1024 * 1024, **kw)


def cost(rows, depth, cols):
    return pl.CostEstimate(flops=2 * rows * depth * cols, bytes_accessed=2 * depth * (cols + rows) + 8 * rows * cols, transcendentals=0)


def pack(blob_ref, state, arrow_t):
    rows, cols = state.shape
    for t in range(cols // TILE):
        blob_ref[t * rows : (t + 1) * rows, :] = state[:, t * TILE : (t + 1) * TILE].astype(BF16)
    if arrow_t is not None:
        base = rows * (cols // TILE)
        half = arrow_t.shape[0] // 2
        blob_ref[base : base + half, :rows] = arrow_t[:half].astype(BF16)
        blob_ref[base : base + half, rows:] = arrow_t[half:].astype(BF16)


def start_kernel(where_ref, own_ref, got_ref, arrow_ref, state_a, state_b, blob_a, blob_b):
    core = where_ref[CHIPS]
    rows = own_ref.shape[0]
    width = state_a.shape[1]
    mine = pl.ds(pl.multiple_of(core * rows, rows), rows)
    theirs = pl.ds(pl.multiple_of((1 - core) * rows, rows), rows)
    for j, state in enumerate((state_a, state_b)):
        column = pl.multiple_of(core * 2 * width + j * width, width)
        state[mine, :] = own_ref[:, pl.ds(column, width)]
        state[theirs, :] = got_ref[:, j * width : (j + 1) * width]
    pack(blob_a, state_a[...], arrow_ref[...])
    pack(blob_b, state_b[...], None)


def fetch(level, maps, pieces, where_ref, map_buf, tile_buf, arrow_buf, sem):
    core = where_ref[CHIPS]
    copies = []

    def go(src, dst):
        copy = pltpu.make_async_copy(src, dst, sem.at[len(copies)])
        copy.start()
        copies.append(copy)

    own, got = maps[: len(maps) // 2], maps[len(maps) // 2 :]
    rows = own[0].shape[2]
    for k in range(len(own)):
        go(own[k].at[0, level], map_buf.at[pl.ds(pl.multiple_of(k * 2 * rows + core * rows, rows), rows)])
        go(got[k].at[0, level], map_buf.at[pl.ds(pl.multiple_of(k * 2 * rows + (1 - core) * rows, rows), rows)])
    tiles = tile_buf.shape[0]
    chunk = 2 * rows
    blob = pieces[0].shape[0] // SIDE
    count = 0
    for piece in pieces:
        for b in range(piece.shape[0] // blob):
            at = pl.multiple_of(where_ref[count], chunk)
            for t in range(tiles):
                go(piece.at[pl.ds(b * blob + t * chunk, chunk)], tile_buf.at[t, pl.ds(at, chunk)])
            if arrow_buf is not None:
                half = arrow_buf.shape[0] // 2
                for h in range(2):
                    go(
                        piece.at[pl.ds(b * blob + tiles * chunk, half), pl.ds(h * chunk, chunk)],
                        arrow_buf.at[pl.ds(h * half, half), pl.ds(at, chunk)],
                    )
            count += 1
    for copy in copies:
        copy.wait()


def schur_kernel(level, last, arrow, n_pieces, *refs):
    where_ref, own, got = refs[:3]
    pieces = refs[3 : 3 + n_pieces]
    rest = list(refs[3 + n_pieces :])
    state = rest.pop(0)
    arrow_in = rest.pop(0) if arrow else None
    outs = [rest.pop(0) for _ in range(2)]
    arrow_out = rest.pop(0) if arrow else None
    map_buf, tile_buf = rest.pop(0), rest.pop(0)
    arrow_buf = rest.pop(0) if arrow else None
    new_state = rest.pop(0) if last else outs[0]
    sem = rest.pop(0)
    fetch(level, (own, got), pieces, where_ref, map_buf, tile_buf, arrow_buf, sem)
    new_arrow = None
    if arrow:
        new_arrow = arrow_in[...] - lax.dot_general(arrow_buf[...], map_buf[...], NT, preferred_element_type=F32)
        arrow_out[...] = new_arrow
    for t in range(tile_buf.shape[0]):
        cols = slice(t * TILE, (t + 1) * TILE)
        new_state[:, cols] = state[:, cols] - jnp.dot(map_buf[...], tile_buf[t], preferred_element_type=F32)
    if last:
        split(where_ref[CHIPS], new_state, 1, outs)
    else:
        pack(outs[1], new_state[...], new_arrow)


def split(core, total, count, outs):
    rows = total.shape[0] // count // 2
    keep, send = outs
    for k in range(count):
        here = slice(k * rows, (k + 1) * rows)
        keep[here, :] = total[pl.ds(pl.multiple_of(k * 2 * rows + core * rows, rows), rows), :]
        send[here, :] = total[pl.ds(pl.multiple_of(k * 2 * rows + (1 - core) * rows, rows), rows), :]


def fill_kernel(level, last, n_pieces, *refs):
    where_ref = refs[0]
    maps = refs[1:7]
    pieces = refs[7 : 7 + n_pieces]
    rest = list(refs[7 + n_pieces :])
    total = rest.pop(0) if level else None
    outs = [rest.pop(0) for _ in range(2 if last else 1)]
    map_buf, tile_buf = rest.pop(0), rest.pop(0)
    new_total = rest.pop(0) if last else outs[0]
    sem = rest.pop(0)
    fetch(level, maps, pieces, where_ref, map_buf, tile_buf, None, sem)
    for t in range(tile_buf.shape[0]):
        cols = slice(t * TILE, (t + 1) * TILE)
        update = jnp.dot(map_buf[...], tile_buf[t], preferred_element_type=F32)
        new_total[:, cols] = update if total is None else total[:, cols] + update
    if last:
        split(where_ref[CHIPS], new_total, 3, outs)


def schur_step(level, last, where, own, got, pieces, state, arrow_t):
    arrow = arrow_t is not None
    rows, cols = state.shape
    depth = own.shape[3]
    tiles = cols // TILE
    blob = rows * tiles + (arrow_t.shape[0] // 2 if arrow else 0)
    shape = jax.ShapeDtypeStruct
    if last:
        out_shape = [shape((rows // 2, cols), F32), shape((rows // 2, cols), F32)]
    else:
        out_shape = [shape((rows, cols), F32), shape((blob, TILE), BF16)]
    scratch = [pltpu.VMEM((rows, depth), BF16), pltpu.VMEM((tiles, depth, TILE), BF16)]
    if arrow:
        out_shape.append(shape(arrow_t.shape, F32))
        scratch.append(pltpu.VMEM((arrow_t.shape[0], depth), BF16))
    if last:
        scratch.append(pltpu.VMEM((rows, cols), F32))
    scratch.append(pltpu.SemaphoreType.DMA((2 + CHIPS * (tiles + (2 if arrow else 0)),)))
    operands = [where, own, got, *pieces, state] + ([arrow_t] if arrow else [])
    return pl.pallas_call(
        functools.partial(schur_kernel, level, last, arrow, len(pieces)),
        out_shape=out_shape,
        in_specs=[SMEM, ANY, ANY] + [ANY] * len(pieces) + [VMEM] * (2 if arrow else 1),
        out_specs=[VMEM] * len(out_shape),
        scratch_shapes=scratch,
        compiler_params=params(),
        cost_estimate=cost(rows, depth, cols),
        name=f"schur_{level}",
    )(*operands)


def fill_step(level, last, where, maps, pieces, rows, cols, total):
    depth = maps[0].shape[3]
    tiles = cols // TILE
    shape = jax.ShapeDtypeStruct
    tall = 3 * rows
    if last:
        out_shape = [shape((tall // 2, cols), F32)] * 2
    else:
        out_shape = [shape((tall, cols), F32)]
    scratch = [pltpu.VMEM((tall, depth), BF16), pltpu.VMEM((tiles, depth, TILE), BF16)]
    if last:
        scratch.append(pltpu.VMEM((tall, cols), F32))
    scratch.append(pltpu.SemaphoreType.DMA((6 + CHIPS * tiles,)))
    operands = [where, *maps, *pieces] + ([total] if level else [])
    return pl.pallas_call(
        functools.partial(fill_kernel, level, last, len(pieces)),
        out_shape=out_shape,
        in_specs=[SMEM] + [ANY] * (6 + len(pieces)) + ([VMEM] if level else []),
        out_specs=[VMEM] * len(out_shape),
        scratch_shapes=scratch,
        compiler_params=params(),
        cost_estimate=cost(tall, depth, cols),
        name=f"fill_{level}",
    )(*operands)


def gather(blob):
    near = [lax.ppermute(blob, "panel", ring(0, step)) for step in (-1, 2, 1)]
    bundle = jnp.concatenate([blob, *near], axis=0)
    ahead = lax.ppermute(bundle, "panel", ring(1, -1))
    behind = lax.ppermute(bundle, "panel", ring(1, 1))
    half = bundle.shape[0] // 2
    far_low = lax.ppermute(behind[:half], "panel", ring(1, 1))
    far_high = lax.ppermute(ahead[half:], "panel", ring(1, -1))
    return [bundle, ahead, far_low, far_high, behind]


def shards(
    boundary,
    far_coupling,
    cross_coupling,
    tail_coupling,
    arrow_block,
    inverse_map,
    fill_map,
    cross_map,
    tail_map,
    arrow_tip,
    inverse_diagonal,
):
    levels = lax.axis_size("tm").bit_length() - 1
    rows, cols = boundary.shape[1:]
    width = cols // 4
    place = lax.axis_index("panel")
    core = place % 2
    y, x = place // 2 // SIDE, place // 2 % SIDE
    second = jnp.arange(CHIPS, dtype=jnp.int32) // SIDE
    first = jnp.arange(CHIPS, dtype=jnp.int32) % SIDE
    up, across = jnp.where(core == 0, second, first), jnp.where(core == 0, first, second)
    order = ((y + up) % SIDE * SIDE + (x + across) % SIDE) * 2 * rows
    where = jnp.concatenate([order.astype(jnp.int32), core.astype(jnp.int32)[None]])

    arrow = arrow_block[0]
    diagonal = inverse_diagonal[0]
    away = jnp.where(core == 0, boundary[0][:, cols // 2 :], boundary[0][:, : cols // 2])
    got = lax.ppermute(jnp.concatenate([away, arrow, diagonal[:, None]], axis=1), "panel", SWAP)
    got_half = got[:, : cols // 2]
    got_arrow = got[:, cols // 2 : cols // 2 + arrow.shape[1]]
    got_diagonal = got[:, -1]

    def paired(mine, theirs, axis):
        return jnp.where(
            core == 0, jnp.concatenate([mine, theirs], axis=axis), jnp.concatenate([theirs, mine], axis=axis)
        )

    arrow_t = paired(arrow.T, got_arrow.T, 1)
    weights = paired(diagonal, got_diagonal, 0)

    maps = (inverse_map, fill_map, cross_map, tail_map)
    got_maps = [lax.ppermute(m, "panel", SWAP) for m in maps]

    shape = jax.ShapeDtypeStruct
    arrow_rows = arrow_t.shape[0] // 2
    state_a, state_b, blob_a, blob_b = pl.pallas_call(
        start_kernel,
        out_shape=[
            shape((2 * rows, width), F32),
            shape((2 * rows, width), F32),
            shape((2 * rows * (width // TILE) + arrow_rows, TILE), BF16),
            shape((2 * rows * (width // TILE), TILE), BF16),
        ],
        in_specs=[SMEM, VMEM, VMEM, VMEM],
        out_specs=[VMEM] * 4,
        compiler_params=params(),
        name="start",
    )(where, boundary[0], got_half, arrow_t)

    states, blobs, totals = [state_a, state_b], [blob_a, blob_b], [None, None]
    kept, sent = [None, None], [None, None]
    fill_maps = [fill_map, cross_map, tail_map, *got_maps[1:]]
    for level in range(levels):
        last = level == levels - 1
        for j in range(2):
            pieces = gather(flip(blobs[j], 1 << level))
            result = schur_step(
                level, last, where, inverse_map, got_maps[0], pieces, states[j], arrow_t if j == 0 else None
            )
            if j == 0:
                arrow_t = result[2]
            filled = fill_step(level, last, where, fill_maps, pieces, 2 * rows, width, totals[j])
            if last:
                kept[j] = (result[0], filled[0])
                sent[j] = (result[1], filled[1])
            else:
                states[j], blobs[j] = result[:2]
                totals[j] = filled[0]

    tip = jnp.dot(arrow_t * weights[None, :], arrow_t.T, precision=lax.Precision.HIGHEST, preferred_element_type=F32)
    for routes in (XOR_X, XOR_Y):
        one, two, three = (lax.ppermute(tip, "panel", routes[k]) for k in (1, 2, 3))
        tip = (tip + one) + (two + three)
    for level in range(levels):
        tip = tip + flip(tip, 1 << level)
    tip_schur = arrow_tip - tip

    back = [[lax.ppermute(part, "panel", SWAP) for part in sent[j]] for j in range(2)]

    def whole(part, k):
        here = slice(k * rows, (k + 1) * rows)
        mine = [kept[j][part][here] for j in range(2)]
        theirs = [back[j][part][here] for j in range(2)]
        return jnp.where(core == 0, jnp.concatenate(mine + theirs, axis=1), jnp.concatenate(theirs + mine, axis=1))

    arrow_cols = jnp.where(core == 0, arrow_t[:, :rows], arrow_t[:, rows:]).T
    return (
        whole(0, 0)[None],
        (far_coupling[0] - whole(1, 0))[None],
        (cross_coupling[0] - whole(1, 1))[None],
        (tail_coupling[0] - whole(1, 2))[None],
        arrow_cols[None],
        tip_schur,
    )


def solution(mesh):
    in_specs = (
        P("tm", "panel", None),
        P("tm", "panel", None),
        P("tm", "panel", None),
        P("tm", "panel", None),
        P("tm", "panel", None),
        P("tm", None, "panel", None),
        P("tm", None, "panel", None),
        P("tm", None, "panel", None),
        P("tm", None, "panel", None),
        P(),
        P("tm", "panel"),
    )
    out_specs = (
        P("tm", "panel", None),
        P("tm", "panel", None),
        P("tm", "panel", None),
        P("tm", "panel", None),
        P("tm", "panel", None),
        P(),
    )
    return jax.shard_map(shards, mesh=mesh, in_specs=in_specs, out_specs=out_specs, check_vma=False)
```

```python
import functools

import jax
import jax.numpy as jnp
from jax import lax
from jax.experimental import pallas as pl
from jax.experimental.pallas import tpu as pltpu
from jax.sharding import PartitionSpec as P

F32 = jnp.float32
BF16 = jnp.bfloat16
SETS = 2
SIDE = 4
CHIPS = SIDE * SIDE
TILE = 256
ANY = pl.BlockSpec(memory_space=pl.ANY)
VMEM = pl.BlockSpec(memory_space=pltpu.VMEM)
SMEM = pl.BlockSpec(memory_space=pltpu.SMEM)
NT = (((1,), (1,)), ((), ()))


def routes(axis, flips):
    out = []
    for y in range(SIDE):
        for x in range(SIDE):
            for core in range(2):
                to_y, to_x = (y, x ^ flips[core]) if axis == 0 else (y ^ flips[core], x)
                out.append(((y * SIDE + x) * 2 + core, (to_y * SIDE + to_x) * 2 + core))
    return out


def ring(first, step):
    out = []
    for y in range(SIDE):
        for x in range(SIDE):
            for core in range(2):
                to_y, to_x = (y, (x + step) % SIDE) if core == first else ((y + step) % SIDE, x)
                out.append(((y * SIDE + x) * 2 + core, (to_y * SIDE + to_x) * 2 + core))
    return out


SWAP = [(i, i ^ 1) for i in range(2 * CHIPS)]


def flip(block, bit):
    count = lax.axis_size("tm")
    return lax.ppermute(block, "tm", [(p, p ^ bit) for p in range(count)])


def params():
    return pltpu.CompilerParams(vmem_limit_bytes=24 * 1024 * 1024)


def cost(rows, depth, cols):
    return pl.CostEstimate(
        flops=2 * rows * depth * cols, bytes_accessed=2 * depth * (cols + rows) + 8 * rows * cols, transcendentals=0
    )


def pack(blob_ref, state, arrow_t):
    rows, cols = state.shape
    for t in range(cols // TILE):
        blob_ref[t * rows : (t + 1) * rows, :] = state[:, t * TILE : (t + 1) * TILE].astype(BF16)
    if arrow_t is not None:
        base = rows * (cols // TILE)
        half = arrow_t.shape[0] // 2
        blob_ref[base : base + half, :rows] = arrow_t[:half].astype(BF16)
        blob_ref[base : base + half, rows:] = arrow_t[half:].astype(BF16)


def start_kernel(where_ref, own_ref, got_ref, arrow_ref, *outs):
    core = where_ref[CHIPS]
    rows = own_ref.shape[0]
    count = len(outs) // 2
    width = outs[0].shape[1]
    mine = pl.ds(pl.multiple_of(core * rows, rows), rows)
    theirs = pl.ds(pl.multiple_of((1 - core) * rows, rows), rows)
    for j in range(count):
        state = outs[j]
        column = pl.multiple_of(core * count * width + j * width, width)
        state[mine, :] = own_ref[:, pl.ds(column, width)]
        state[theirs, :] = got_ref[:, j * width : (j + 1) * width]
        pack(outs[count + j], state[...], arrow_ref[...] if j == 0 else None)


def load_maps(level, own, got, where_ref, raw, ordered, sem):
    core = where_ref[CHIPS]
    rows = own[0].shape[2]
    copies = []
    for k in range(len(own)):
        for at, ref in ((core, own[k]), (1 - core, got[k])):
            at = pl.ds(pl.multiple_of((2 * k + at) * rows, rows), rows)
            copies.append(pltpu.make_async_copy(ref.at[0, level], raw.at[at], sem.at[len(copies)]))
    for copy in copies:
        copy.start()
    for copy in copies:
        copy.wait()
    chunk = 2 * rows
    for k in range(CHIPS):
        at = pl.multiple_of(where_ref[k], chunk)
        ordered[:, k * chunk : (k + 1) * chunk] = raw[:, pl.ds(at, chunk)]


def tile_of(bundle, blob, chunk, t):
    count = bundle.shape[0] // blob
    if blob == chunk:
        return bundle[...]
    return jnp.concatenate([bundle[k * blob + t * chunk : k * blob + (t + 1) * chunk, :] for k in range(count)], axis=0)


def product(ordered, bundles, blob, chunk, t):
    total = None
    start = 0
    for bundle in bundles:
        depth = bundle.shape[0] // blob * chunk
        term = jnp.dot(
            ordered[:, start : start + depth], tile_of(bundle, blob, chunk, t), preferred_element_type=F32
        )
        total = term if total is None else total + term
        start += depth
    return total


def schur_kernel(level, last, arrow, late, *refs):
    refs = list(refs)
    where_ref, own, got = refs[:3]
    bundles = refs[3 : 3 + SIDE]
    state = refs[3 + SIDE]
    refs = refs[4 + SIDE :]
    arrow_in = refs.pop(0) if arrow else None
    if late:
        refs.pop(0)
    outs = [refs.pop(0) for _ in range(2)]
    arrow_out = refs.pop(0) if arrow else None
    raw, ordered = refs.pop(0), refs.pop(0)
    arrow_buf = refs.pop(0) if arrow else None
    new_state = refs.pop(0) if last else outs[0]
    sem = refs.pop(0)
    load_maps(level, (own,), (got,), where_ref, raw, ordered, sem)
    chunk, cols = state.shape
    tiles = cols // TILE
    blob = bundles[0].shape[0] // SIDE
    new_arrow = None
    if arrow:
        half = arrow_in.shape[0] // 2
        for k in range(CHIPS):
            bundle, at = bundles[k // SIDE], k % SIDE * blob + tiles * chunk
            for h in range(2):
                arrow_buf[h * half : (h + 1) * half, k * chunk : (k + 1) * chunk] = bundle[
                    at : at + half, h * chunk : (h + 1) * chunk
                ]
        new_arrow = arrow_in[...] - lax.dot_general(arrow_buf[...], ordered[...], NT, preferred_element_type=F32)
        arrow_out[...] = new_arrow
    for t in range(tiles):
        columns = slice(t * TILE, (t + 1) * TILE)
        new_state[:, columns] = state[:, columns] - product(ordered, bundles, blob, chunk, t)
    if last:
        split(where_ref[CHIPS], new_state, 1, outs)
    else:
        pack(outs[1], new_state[...], new_arrow)


def split(core, total, count, outs):
    rows = total.shape[0] // count // 2
    keep, send = outs
    for k in range(count):
        here = slice(k * rows, (k + 1) * rows)
        keep[here, :] = total[pl.ds(pl.multiple_of((2 * k + core) * rows, rows), rows), :]
        send[here, :] = total[pl.ds(pl.multiple_of((2 * k + 1 - core) * rows, rows), rows), :]


def fill_kernel(level, last, *refs):
    refs = list(refs)
    where_ref = refs[0]
    own, got = refs[1:4], refs[4:7]
    bundles = refs[7 : 7 + SIDE]
    refs = refs[8 + SIDE :]
    total = refs.pop(0) if level else None
    outs = [refs.pop(0) for _ in range(2 if last else 1)]
    raw, ordered = refs.pop(0), refs.pop(0)
    new_total = refs.pop(0) if last else outs[0]
    sem = refs.pop(0)
    load_maps(level, own, got, where_ref, raw, ordered, sem)
    chunk = 2 * own[0].shape[2]
    blob = bundles[0].shape[0] // SIDE
    for t in range(new_total.shape[1] // TILE):
        columns = slice(t * TILE, (t + 1) * TILE)
        update = product(ordered, bundles, blob, chunk, t)
        new_total[:, columns] = update if total is None else total[:, columns] + update
    if last:
        split(where_ref[CHIPS], new_total, 3, outs)


def schur_step(level, last, where, own, got, bundles, state, arrow_t, after):
    arrow = arrow_t is not None
    rows, cols = state.shape
    depth = own.shape[3]
    blob = bundles[0].shape[0] // SIDE
    shape = jax.ShapeDtypeStruct
    if last:
        out_shape = [shape((rows // 2, cols), F32)] * 2
    else:
        out_shape = [shape((rows, cols), F32), shape((blob, TILE), BF16)]
    scratch = [pltpu.VMEM((rows, depth), BF16)] * 2
    if arrow:
        out_shape.append(shape(arrow_t.shape, F32))
        scratch.append(pltpu.VMEM((arrow_t.shape[0], depth), BF16))
    if last:
        scratch.append(pltpu.VMEM((rows, cols), F32))
    scratch.append(pltpu.SemaphoreType.DMA((2,)))
    late = [] if after is None else [after]
    operands = [where, own, got, *bundles, state] + ([arrow_t] if arrow else []) + late
    return pl.pallas_call(
        functools.partial(schur_kernel, level, last, arrow, len(late)),
        out_shape=out_shape,
        in_specs=[SMEM, ANY, ANY] + [VMEM] * (SIDE + (2 if arrow else 1)) + [ANY] * len(late),
        out_specs=[VMEM] * len(out_shape),
        scratch_shapes=scratch,
        compiler_params=params(),
        cost_estimate=cost(rows, depth, cols),
        name=f"schur_{level}",
    )(*operands)


def fill_step(level, last, where, maps, bundles, rows, cols, total, after):
    depth = maps[0].shape[3]
    shape = jax.ShapeDtypeStruct
    tall = 3 * rows
    if last:
        out_shape = [shape((tall // 2, cols), F32)] * 2
    else:
        out_shape = [shape((tall, cols), F32)]
    scratch = [pltpu.VMEM((tall, depth), BF16)] * 2
    if last:
        scratch.append(pltpu.VMEM((tall, cols), F32))
    scratch.append(pltpu.SemaphoreType.DMA((6,)))
    operands = [where, *maps, *bundles, after] + ([total] if level else [])
    return pl.pallas_call(
        functools.partial(fill_kernel, level, last),
        out_shape=out_shape,
        in_specs=[SMEM] + [ANY] * 6 + [VMEM] * SIDE + [ANY] + [VMEM] * (1 if level else 0),
        out_specs=[VMEM] * len(out_shape),
        scratch_shapes=scratch,
        compiler_params=params(),
        cost_estimate=cost(tall, depth, cols),
        name=f"fill_{level}",
    )(*operands)


def around(block, first):
    return [lax.ppermute(block, "panel", ring(first, step)) for step in (-1, 2, 1)]


def every_partition(tip, core):
    count = lax.axis_size("tm")
    half = count // 2
    width = lax.axis_size("panel")
    parts = [tip]
    for k in range(half):
        pairs = []
        for p in range(count):
            for i in range(width):
                away = k if i % 2 == 0 else half + k
                if away:
                    pairs.append((p * width + i, (p ^ away) * width + i))
        parts.append(lax.ppermute(tip, ("tm", "panel"), pairs))
    parts = [jnp.where(core == 0, tip, parts[1]), *parts[2:]]
    while len(parts) > 1:
        parts = [parts[i] + parts[i + 1] for i in range(0, len(parts), 2)]
    return parts[0] + lax.ppermute(parts[0], "panel", SWAP)


def shards(
    boundary,
    far_coupling,
    cross_coupling,
    tail_coupling,
    arrow_block,
    inverse_map,
    fill_map,
    cross_map,
    tail_map,
    arrow_tip,
    inverse_diagonal,
):
    levels = lax.axis_size("tm").bit_length() - 1
    rows, cols = boundary.shape[1:]
    chunk = 2 * rows
    count = SETS
    width = cols // 2 // count
    place = lax.axis_index("panel")
    core = place % 2
    y, x = place // 2 // SIDE, place // 2 % SIDE
    number = jnp.arange(CHIPS, dtype=jnp.int32)
    inner, outer = number % SIDE, number // SIDE
    up, across = jnp.where(core == 0, outer, inner), jnp.where(core == 0, inner, outer)
    order = ((y + up) % SIDE * SIDE + (x + across) % SIDE) * chunk
    where = jnp.concatenate([order, core[None]]).astype(jnp.int32)

    arrow = arrow_block[0]
    diagonal = inverse_diagonal[0]
    away = jnp.where(core == 0, boundary[0][:, cols // 2 :], boundary[0][:, : cols // 2])
    got = lax.ppermute(jnp.concatenate([away, arrow, diagonal[:, None]], axis=1), "panel", SWAP)
    got_half = got[:, : cols // 2]
    got_arrow = got[:, cols // 2 : cols // 2 + arrow.shape[1]]
    got_diagonal = got[:, -1]

    def paired(mine, theirs, axis):
        return jnp.where(
            core == 0, jnp.concatenate([mine, theirs], axis=axis), jnp.concatenate([theirs, mine], axis=axis)
        )

    arrow_t = paired(arrow.T, got_arrow.T, 1)
    weights = paired(diagonal, got_diagonal, 0)

    maps = (inverse_map, fill_map, cross_map, tail_map)
    got_maps = [lax.ppermute(m, "panel", SWAP) for m in maps]
    fill_maps = [*maps[1:], *got_maps[1:]]

    shape = jax.ShapeDtypeStruct
    extra = [arrow_t.shape[0] // 2] + [0] * (count - 1)
    begun = pl.pallas_call(
        start_kernel,
        out_shape=[shape((chunk, width), F32)] * count
        + [shape((chunk * (width // TILE) + more, TILE), BF16) for more in extra],
        in_specs=[SMEM, VMEM, VMEM, VMEM],
        out_specs=[VMEM] * (2 * count),
        compiler_params=params(),
        name="start",
    )(where, boundary[0], got_half, arrow_t)

    states, blobs, totals = list(begun[:count]), list(begun[count:]), [None] * count
    kept, sent = [None] * count, [None] * count
    def begin(blob, level, total):
        got = flip(blob, 1 << level)
        if total is not None:
            got, total = lax.optimization_barrier((got, total))
        return jnp.concatenate([got, *around(got, 0)], axis=0), total

    bundles = [None] * count
    for j in range(count):
        bundles[j], _ = begin(blobs[j], 0, None)
    for level in range(levels):
        last = level == levels - 1
        for j in range(count):
            pieces = [bundles[j], *around(bundles[j], 1)]
            other = None if (j == 0 and level == 0) else bundles[(j + 1) % count]
            if last and j == count - 1:
                other = None
            result = schur_step(
                level, last, where, inverse_map, got_maps[0], pieces, states[j], arrow_t if j == 0 else None, other
            )
            if j == 0:
                arrow_t = result[2]
            filled = fill_step(level, last, where, fill_maps, pieces, chunk, width, totals[j], result[1])
            if last:
                kept[j] = jnp.concatenate([result[0], filled[0]], axis=0)
                sent[j] = jnp.concatenate([result[1], filled[1]], axis=0)
            else:
                states[j] = result[0]
                bundles[j], totals[j] = begin(result[1], level + 1, filled[0])

    tip = jnp.dot(arrow_t * weights[None, :], arrow_t.T, precision=lax.Precision.HIGHEST, preferred_element_type=F32)
    for axis in range(2):
        first, second, third = (lax.ppermute(tip, "panel", routes(axis, (k, k))) for k in (1, 2, 3))
        tip = (tip + first) + (second + third)
    tip, sent[-1] = lax.optimization_barrier((tip, sent[-1]))
    tip = every_partition(tip, core)
    tip_schur = arrow_tip - tip

    back = [lax.ppermute(part, "panel", SWAP) for part in sent]

    def whole(k):
        here = slice(k * rows, (k + 1) * rows)
        mine = [part[here] for part in kept]
        theirs = [part[here] for part in back]
        return jnp.where(core == 0, jnp.concatenate(mine + theirs, axis=1), jnp.concatenate(theirs + mine, axis=1))

    arrow_cols = jnp.where(core == 0, arrow_t[:, :rows], arrow_t[:, rows:]).T
    return (
        whole(0)[None],
        (far_coupling[0] - whole(1))[None],
        (cross_coupling[0] - whole(2))[None],
        (tail_coupling[0] - whole(3))[None],
        arrow_cols[None],
        tip_schur,
    )
def solution(mesh):
    in_specs = (
        P("tm", "panel", None),
        P("tm", "panel", None),
        P("tm", "panel", None),
        P("tm", "panel", None),
        P("tm", "panel", None),
        P("tm", None, "panel", None),
        P("tm", None, "panel", None),
        P("tm", None, "panel", None),
        P("tm", None, "panel", None),
        P(),
        P("tm", "panel"),
    )
    out_specs = (
        P("tm", "panel", None),
        P("tm", "panel", None),
        P("tm", "panel", None),
        P("tm", "panel", None),
        P("tm", "panel", None),
        P(),
    )
    return jax.shard_map(shards, mesh=mesh, in_specs=in_specs, out_specs=out_specs, check_vma=False)
```

```python
import functools

import jax
import jax.numpy as jnp
from jax import lax
from jax.experimental import pallas as pl
from jax.experimental.pallas import tpu as pltpu
from jax.sharding import PartitionSpec as P

F32 = jnp.float32
BF16 = jnp.bfloat16
SETS = 2
SIDE = 4
CHIPS = SIDE * SIDE
TILE = 256
ANY = pl.BlockSpec(memory_space=pl.ANY)
VMEM = pl.BlockSpec(memory_space=pltpu.VMEM)
SMEM = pl.BlockSpec(memory_space=pltpu.SMEM)
NT = (((1,), (1,)), ((), ()))


def routes(axis, flips):
    out = []
    for y in range(SIDE):
        for x in range(SIDE):
            for core in range(2):
                to_y, to_x = (y, x ^ flips[core]) if axis == 0 else (y ^ flips[core], x)
                out.append(((y * SIDE + x) * 2 + core, (to_y * SIDE + to_x) * 2 + core))
    return out


def ring(first, step):
    out = []
    for y in range(SIDE):
        for x in range(SIDE):
            for core in range(2):
                to_y, to_x = (y, (x + step) % SIDE) if core == first else ((y + step) % SIDE, x)
                out.append(((y * SIDE + x) * 2 + core, (to_y * SIDE + to_x) * 2 + core))
    return out


SWAP = [(i, i ^ 1) for i in range(2 * CHIPS)]


def flip(block, bit):
    count = lax.axis_size("tm")
    return lax.ppermute(block, "tm", [(p, p ^ bit) for p in range(count)])


def params():
    return pltpu.CompilerParams(vmem_limit_bytes=24 * 1024 * 1024)


def cost(rows, depth, cols):
    return pl.CostEstimate(
        flops=2 * rows * depth * cols, bytes_accessed=2 * depth * (cols + rows) + 8 * rows * cols, transcendentals=0
    )


def pack(blob_ref, state, arrow_t):
    rows, cols = state.shape
    for t in range(cols // TILE):
        blob_ref[t * rows : (t + 1) * rows, :] = state[:, t * TILE : (t + 1) * TILE].astype(BF16)
    if arrow_t is not None:
        base = rows * (cols // TILE)
        half = arrow_t.shape[0] // 2
        blob_ref[base : base + half, :rows] = arrow_t[:half].astype(BF16)
        blob_ref[base : base + half, rows:] = arrow_t[half:].astype(BF16)


def start_kernel(where_ref, own_ref, got_ref, arrow_ref, *outs):
    core = where_ref[CHIPS]
    rows = own_ref.shape[0]
    count = len(outs) // 2
    width = outs[0].shape[1]
    mine = pl.ds(pl.multiple_of(core * rows, rows), rows)
    theirs = pl.ds(pl.multiple_of((1 - core) * rows, rows), rows)
    for j in range(count):
        state = outs[j]
        column = pl.multiple_of(core * count * width + j * width, width)
        state[mine, :] = own_ref[:, pl.ds(column, width)]
        state[theirs, :] = got_ref[:, j * width : (j + 1) * width]
        pack(outs[count + j], state[...], arrow_ref[...] if j == 0 else None)


def load_maps(level, own, got, where_ref, raw, ordered, sem):
    core = where_ref[CHIPS]
    rows = own[0].shape[2]
    copies = []
    for k in range(len(own)):
        for at, ref in ((core, own[k]), (1 - core, got[k])):
            at = pl.ds(pl.multiple_of((2 * k + at) * rows, rows), rows)
            copies.append(pltpu.make_async_copy(ref.at[0, level], raw.at[at], sem.at[len(copies)]))
    for copy in copies:
        copy.start()
    for copy in copies:
        copy.wait()
    chunk = 2 * rows
    for k in range(CHIPS):
        at = pl.multiple_of(where_ref[k], chunk)
        ordered[:, k * chunk : (k + 1) * chunk] = raw[:, pl.ds(at, chunk)]


def tile_of(bundle, blob, chunk, t):
    count = bundle.shape[0] // blob
    if blob == chunk:
        return bundle[...]
    return jnp.concatenate([bundle[k * blob + t * chunk : k * blob + (t + 1) * chunk, :] for k in range(count)], axis=0)


def product(ordered, bundles, blob, chunk, t):
    total = None
    start = 0
    for bundle in bundles:
        depth = bundle.shape[0] // blob * chunk
        term = jnp.dot(
            ordered[:, start : start + depth], tile_of(bundle, blob, chunk, t), preferred_element_type=F32
        )
        total = term if total is None else total + term
        start += depth
    return total


def schur_kernel(level, last, arrow, late, *refs):
    refs = list(refs)
    where_ref, own, got = refs[:3]
    bundles = refs[3 : 3 + SIDE]
    state = refs[3 + SIDE]
    refs = refs[4 + SIDE :]
    arrow_in = refs.pop(0) if arrow else None
    if late:
        refs.pop(0)
    outs = [refs.pop(0) for _ in range(2)]
    arrow_out = refs.pop(0) if arrow else None
    raw, ordered = refs.pop(0), refs.pop(0)
    arrow_buf = refs.pop(0) if arrow else None
    new_state = refs.pop(0) if last else outs[0]
    sem = refs.pop(0)
    load_maps(level, (own,), (got,), where_ref, raw, ordered, sem)
    chunk, cols = state.shape
    tiles = cols // TILE
    blob = bundles[0].shape[0] // SIDE
    new_arrow = None
    if arrow:
        half = arrow_in.shape[0] // 2
        for k in range(CHIPS):
            bundle, at = bundles[k // SIDE], k % SIDE * blob + tiles * chunk
            for h in range(2):
                arrow_buf[h * half : (h + 1) * half, k * chunk : (k + 1) * chunk] = bundle[
                    at : at + half, h * chunk : (h + 1) * chunk
                ]
        new_arrow = arrow_in[...] - lax.dot_general(arrow_buf[...], ordered[...], NT, preferred_element_type=F32)
        arrow_out[...] = new_arrow
    for t in range(tiles):
        columns = slice(t * TILE, (t + 1) * TILE)
        new_state[:, columns] = state[:, columns] - product(ordered, bundles, blob, chunk, t)
    if last:
        split(where_ref[CHIPS], new_state, 1, outs)
    else:
        pack(outs[1], new_state[...], new_arrow)


def split(core, total, count, outs):
    rows = total.shape[0] // count // 2
    keep, send = outs
    for k in range(count):
        here = slice(k * rows, (k + 1) * rows)
        keep[here, :] = total[pl.ds(pl.multiple_of((2 * k + core) * rows, rows), rows), :]
        send[here, :] = total[pl.ds(pl.multiple_of((2 * k + 1 - core) * rows, rows), rows), :]


def fill_kernel(level, last, *refs):
    refs = list(refs)
    where_ref = refs[0]
    own, got = refs[1:4], refs[4:7]
    bundles = refs[7 : 7 + SIDE]
    refs = refs[8 + SIDE :]
    total = refs.pop(0) if level else None
    outs = [refs.pop(0) for _ in range(2 if last else 1)]
    raw, ordered = refs.pop(0), refs.pop(0)
    new_total = refs.pop(0) if last else outs[0]
    sem = refs.pop(0)
    load_maps(level, own, got, where_ref, raw, ordered, sem)
    chunk = 2 * own[0].shape[2]
    blob = bundles[0].shape[0] // SIDE
    for t in range(new_total.shape[1] // TILE):
        columns = slice(t * TILE, (t + 1) * TILE)
        update = product(ordered, bundles, blob, chunk, t)
        new_total[:, columns] = update if total is None else total[:, columns] + update
    if last:
        split(where_ref[CHIPS], new_total, 3, outs)


def schur_step(level, last, where, own, got, bundles, state, arrow_t, after):
    arrow = arrow_t is not None
    rows, cols = state.shape
    depth = own.shape[3]
    blob = bundles[0].shape[0] // SIDE
    shape = jax.ShapeDtypeStruct
    if last:
        out_shape = [shape((rows // 2, cols), F32)] * 2
    else:
        out_shape = [shape((rows, cols), F32), shape((blob, TILE), BF16)]
    scratch = [pltpu.VMEM((rows, depth), BF16)] * 2
    if arrow:
        out_shape.append(shape(arrow_t.shape, F32))
        scratch.append(pltpu.VMEM((arrow_t.shape[0], depth), BF16))
    if last:
        scratch.append(pltpu.VMEM((rows, cols), F32))
    scratch.append(pltpu.SemaphoreType.DMA((2,)))
    late = [] if after is None else [after]
    operands = [where, own, got, *bundles, state] + ([arrow_t] if arrow else []) + late
    return pl.pallas_call(
        functools.partial(schur_kernel, level, last, arrow, len(late)),
        out_shape=out_shape,
        in_specs=[SMEM, ANY, ANY] + [VMEM] * (SIDE + (2 if arrow else 1)) + [ANY] * len(late),
        out_specs=[VMEM] * len(out_shape),
        scratch_shapes=scratch,
        compiler_params=params(),
        cost_estimate=cost(rows, depth, cols),
        name=f"schur_{level}",
    )(*operands)


def fill_step(level, last, where, maps, bundles, rows, cols, total, after):
    depth = maps[0].shape[3]
    shape = jax.ShapeDtypeStruct
    tall = 3 * rows
    if last:
        out_shape = [shape((tall // 2, cols), F32)] * 2
    else:
        out_shape = [shape((tall, cols), F32)]
    scratch = [pltpu.VMEM((tall, depth), BF16)] * 2
    if last:
        scratch.append(pltpu.VMEM((tall, cols), F32))
    scratch.append(pltpu.SemaphoreType.DMA((6,)))
    operands = [where, *maps, *bundles, after] + ([total] if level else [])
    return pl.pallas_call(
        functools.partial(fill_kernel, level, last),
        out_shape=out_shape,
        in_specs=[SMEM] + [ANY] * 6 + [VMEM] * SIDE + [ANY] + [VMEM] * (1 if level else 0),
        out_specs=[VMEM] * len(out_shape),
        scratch_shapes=scratch,
        compiler_params=params(),
        cost_estimate=cost(tall, depth, cols),
        name=f"fill_{level}",
    )(*operands)


def around(block, first):
    return [lax.ppermute(block, "panel", ring(first, step)) for step in (-1, 2, 1)]


def every_partition(tip, core, blocks):
    count = lax.axis_size("tm")
    half = count // 2
    width = lax.axis_size("panel")
    parts = [tip]
    for k in range(half):
        pairs = []
        for p in range(count):
            for i in range(width):
                away = k if i % 2 == 0 else half + k
                if away:
                    pairs.append((p * width + i, (p ^ away) * width + i))
        parts.append(lax.ppermute(tip, ("tm", "panel"), pairs))
    parts, blocks = lax.optimization_barrier((parts, blocks))
    parts = [jnp.where(core == 0, parts[0], parts[1]), *parts[2:]]
    while len(parts) > 1:
        parts = [parts[i] + parts[i + 1] for i in range(0, len(parts), 2)]
    return parts[0] + lax.ppermute(parts[0], "panel", SWAP), blocks


def shards(
    boundary,
    far_coupling,
    cross_coupling,
    tail_coupling,
    arrow_block,
    inverse_map,
    fill_map,
    cross_map,
    tail_map,
    arrow_tip,
    inverse_diagonal,
):
    levels = lax.axis_size("tm").bit_length() - 1
    rows, cols = boundary.shape[1:]
    chunk = 2 * rows
    count = SETS
    width = cols // 2 // count
    place = lax.axis_index("panel")
    core = place % 2
    y, x = place // 2 // SIDE, place // 2 % SIDE
    number = jnp.arange(CHIPS, dtype=jnp.int32)
    inner, outer = number % SIDE, number // SIDE
    up, across = jnp.where(core == 0, outer, inner), jnp.where(core == 0, inner, outer)
    order = ((y + up) % SIDE * SIDE + (x + across) % SIDE) * chunk
    where = jnp.concatenate([order, core[None]]).astype(jnp.int32)

    arrow = arrow_block[0]
    diagonal = inverse_diagonal[0]
    away = jnp.where(core == 0, boundary[0][:, cols // 2 :], boundary[0][:, : cols // 2])
    got = lax.ppermute(jnp.concatenate([away, arrow, diagonal[:, None]], axis=1), "panel", SWAP)
    got_half = got[:, : cols // 2]
    got_arrow = got[:, cols // 2 : cols // 2 + arrow.shape[1]]
    got_diagonal = got[:, -1]

    def paired(mine, theirs, axis):
        return jnp.where(
            core == 0, jnp.concatenate([mine, theirs], axis=axis), jnp.concatenate([theirs, mine], axis=axis)
        )

    arrow_t = paired(arrow.T, got_arrow.T, 1)
    weights = paired(diagonal, got_diagonal, 0)

    maps = (inverse_map, fill_map, cross_map, tail_map)
    got_maps = [lax.ppermute(m, "panel", SWAP) for m in maps]
    fill_maps = [*maps[1:], *got_maps[1:]]

    shape = jax.ShapeDtypeStruct
    extra = [arrow_t.shape[0] // 2] + [0] * (count - 1)
    begun = pl.pallas_call(
        start_kernel,
        out_shape=[shape((chunk, width), F32)] * count
        + [shape((chunk * (width // TILE) + more, TILE), BF16) for more in extra],
        in_specs=[SMEM, VMEM, VMEM, VMEM],
        out_specs=[VMEM] * (2 * count),
        compiler_params=params(),
        name="start",
    )(where, boundary[0], got_half, arrow_t)

    states, blobs, totals = list(begun[:count]), list(begun[count:]), [None] * count
    kept, sent = [None] * count, [None] * count
    def begin(blob, level, total):
        got = flip(blob, 1 << level)
        if total is not None:
            got, total = lax.optimization_barrier((got, total))
        return jnp.concatenate([got, *around(got, 0)], axis=0), total

    bundles = [None] * count
    for j in range(count):
        bundles[j], _ = begin(blobs[j], 0, None)
    for level in range(levels):
        last = level == levels - 1
        for j in range(count):
            pieces = [bundles[j], *around(bundles[j], 1)]
            other = None if (j == 0 and level == 0) else bundles[(j + 1) % count]
            if last and j == count - 1:
                other = None
            result = schur_step(
                level, last, where, inverse_map, got_maps[0], pieces, states[j], arrow_t if j == 0 else None, other
            )
            if j == 0:
                arrow_t = result[2]
            filled = fill_step(level, last, where, fill_maps, pieces, chunk, width, totals[j], result[1])
            if last:
                kept[j] = jnp.concatenate([result[0], filled[0]], axis=0)
                sent[j] = jnp.concatenate([result[1], filled[1]], axis=0)
            else:
                states[j] = result[0]
                bundles[j], totals[j] = begin(result[1], level + 1, filled[0])

    tip = jnp.dot(arrow_t * weights[None, :], arrow_t.T, precision=lax.Precision.HIGHEST, preferred_element_type=F32)
    for axis in range(2):
        first, second, third = (lax.ppermute(tip, "panel", routes(axis, (k, k))) for k in (1, 2, 3))
        tip = (tip + first) + (second + third)
    back = [lax.ppermute(part, "panel", SWAP) for part in sent]
    tip, back[-1] = lax.optimization_barrier((tip, back[-1]))

    def whole(k):
        here = slice(k * rows, (k + 1) * rows)
        mine = [part[here] for part in kept]
        theirs = [part[here] for part in back]
        return jnp.where(core == 0, jnp.concatenate(mine + theirs, axis=1), jnp.concatenate(theirs + mine, axis=1))

    arrow_cols = jnp.where(core == 0, arrow_t[:, :rows], arrow_t[:, rows:]).T
    blocks = [
        whole(0),
        far_coupling[0] - whole(1),
        cross_coupling[0] - whole(2),
        tail_coupling[0] - whole(3),
        arrow_cols,
    ]
    tip, blocks = every_partition(tip, core, blocks)
    return (*(block[None] for block in blocks), arrow_tip - tip)


def solution(mesh):
    in_specs = (
        P("tm", "panel", None),
        P("tm", "panel", None),
        P("tm", "panel", None),
        P("tm", "panel", None),
        P("tm", "panel", None),
        P("tm", None, "panel", None),
        P("tm", None, "panel", None),
        P("tm", None, "panel", None),
        P("tm", None, "panel", None),
        P(),
        P("tm", "panel"),
    )
    out_specs = (
        P("tm", "panel", None),
        P("tm", "panel", None),
        P("tm", "panel", None),
        P("tm", "panel", None),
        P("tm", "panel", None),
        P(),
    )
    return jax.shard_map(shards, mesh=mesh, in_specs=in_specs, out_specs=out_specs, check_vma=False)
```

```python
import functools

import jax
import jax.numpy as jnp
from jax import lax
from jax.experimental import pallas as pl
from jax.experimental.pallas import tpu as pltpu
from jax.sharding import PartitionSpec as P

F32 = jnp.float32
BF16 = jnp.bfloat16
SETS = 2
SIDE = 4
CHIPS = SIDE * SIDE
TILE = 256
ANY = pl.BlockSpec(memory_space=pl.ANY)
VMEM = pl.BlockSpec(memory_space=pltpu.VMEM)
SMEM = pl.BlockSpec(memory_space=pltpu.SMEM)
NT = (((1,), (1,)), ((), ()))


def routes(axis, flips):
    out = []
    for y in range(SIDE):
        for x in range(SIDE):
            for core in range(2):
                to_y, to_x = (y, x ^ flips[core]) if axis == 0 else (y ^ flips[core], x)
                out.append(((y * SIDE + x) * 2 + core, (to_y * SIDE + to_x) * 2 + core))
    return out


def ring(first, step):
    out = []
    for y in range(SIDE):
        for x in range(SIDE):
            for core in range(2):
                to_y, to_x = (y, (x + step) % SIDE) if core == first else ((y + step) % SIDE, x)
                out.append(((y * SIDE + x) * 2 + core, (to_y * SIDE + to_x) * 2 + core))
    return out


SWAP = [(i, i ^ 1) for i in range(2 * CHIPS)]


def flip(block, bit):
    count = lax.axis_size("tm")
    return lax.ppermute(block, "tm", [(p, p ^ bit) for p in range(count)])


def params():
    return pltpu.CompilerParams(vmem_limit_bytes=24 * 1024 * 1024)


def cost(rows, depth, cols):
    return pl.CostEstimate(
        flops=2 * rows * depth * cols, bytes_accessed=2 * depth * (cols + rows) + 8 * rows * cols, transcendentals=0
    )


def pack(blob_ref, state, arrow_t):
    rows, cols = state.shape
    for t in range(cols // TILE):
        blob_ref[t * rows : (t + 1) * rows, :] = state[:, t * TILE : (t + 1) * TILE].astype(BF16)
    if arrow_t is not None:
        base = rows * (cols // TILE)
        half = arrow_t.shape[0] // 2
        blob_ref[base : base + half, :rows] = arrow_t[:half].astype(BF16)
        blob_ref[base : base + half, rows:] = arrow_t[half:].astype(BF16)


def start_kernel(where_ref, own_ref, got_ref, arrow_ref, *outs):
    core = where_ref[CHIPS]
    rows = own_ref.shape[0]
    count = len(outs) // 2
    width = outs[0].shape[1]
    mine = pl.ds(pl.multiple_of(core * rows, rows), rows)
    theirs = pl.ds(pl.multiple_of((1 - core) * rows, rows), rows)
    for j in range(count):
        state = outs[j]
        column = pl.multiple_of(core * count * width + j * width, width)
        state[mine, :] = own_ref[:, pl.ds(column, width)]
        state[theirs, :] = got_ref[:, j * width : (j + 1) * width]
        pack(outs[count + j], state[...], arrow_ref[...] if j == 0 else None)


def load_maps(level, own, got, where_ref, raw, ordered, sem):
    core = where_ref[CHIPS]
    rows = own[0].shape[2]
    copies = []
    for k in range(len(own)):
        for at, ref in ((core, own[k]), (1 - core, got[k])):
            at = pl.ds(pl.multiple_of((2 * k + at) * rows, rows), rows)
            copies.append(pltpu.make_async_copy(ref.at[0, level], raw.at[at], sem.at[len(copies)]))
    for copy in copies:
        copy.start()
    for copy in copies:
        copy.wait()
    chunk = 2 * rows
    for k in range(CHIPS):
        at = pl.multiple_of(where_ref[k], chunk)
        ordered[:, k * chunk : (k + 1) * chunk] = raw[:, pl.ds(at, chunk)]


def tile_of(bundle, blob, chunk, t):
    count = bundle.shape[0] // blob
    if blob == chunk:
        return bundle[...]
    return jnp.concatenate([bundle[k * blob + t * chunk : k * blob + (t + 1) * chunk, :] for k in range(count)], axis=0)


def product(ordered, bundles, blob, chunk, t):
    total = None
    start = 0
    for bundle in bundles:
        depth = bundle.shape[0] // blob * chunk
        term = jnp.dot(
            ordered[:, start : start + depth], tile_of(bundle, blob, chunk, t), preferred_element_type=F32
        )
        total = term if total is None else total + term
        start += depth
    return total


def schur_kernel(level, last, arrow, late, *refs):
    refs = list(refs)
    where_ref, own, got = refs[:3]
    bundles = refs[3 : 3 + SIDE]
    state = refs[3 + SIDE]
    refs = refs[4 + SIDE :]
    arrow_in = refs.pop(0) if arrow else None
    if late:
        refs.pop(0)
    outs = [refs.pop(0) for _ in range(2)]
    arrow_out = refs.pop(0) if arrow else None
    raw, ordered = refs.pop(0), refs.pop(0)
    arrow_buf = refs.pop(0) if arrow else None
    new_state = refs.pop(0) if last else outs[0]
    sem = refs.pop(0)
    load_maps(level, (own,), (got,), where_ref, raw, ordered, sem)
    chunk, cols = state.shape
    tiles = cols // TILE
    blob = bundles[0].shape[0] // SIDE
    new_arrow = None
    if arrow:
        half = arrow_in.shape[0] // 2
        for k in range(CHIPS):
            bundle, at = bundles[k // SIDE], k % SIDE * blob + tiles * chunk
            for h in range(2):
                arrow_buf[h * half : (h + 1) * half, k * chunk : (k + 1) * chunk] = bundle[
                    at : at + half, h * chunk : (h + 1) * chunk
                ]
        new_arrow = arrow_in[...] - lax.dot_general(arrow_buf[...], ordered[...], NT, preferred_element_type=F32)
        arrow_out[...] = new_arrow
    for t in range(tiles):
        columns = slice(t * TILE, (t + 1) * TILE)
        new_state[:, columns] = state[:, columns] - product(ordered, bundles, blob, chunk, t)
    if last:
        split(where_ref[CHIPS], new_state, 1, outs)
    else:
        pack(outs[1], new_state[...], new_arrow)


def split(core, total, count, outs):
    rows = total.shape[0] // count // 2
    keep, send = outs
    for k in range(count):
        here = slice(k * rows, (k + 1) * rows)
        keep[here, :] = total[pl.ds(pl.multiple_of((2 * k + core) * rows, rows), rows), :]
        send[here, :] = total[pl.ds(pl.multiple_of((2 * k + 1 - core) * rows, rows), rows), :]


def fill_kernel(level, last, *refs):
    refs = list(refs)
    where_ref = refs[0]
    own, got = refs[1:4], refs[4:7]
    bundles = refs[7 : 7 + SIDE]
    refs = refs[8 + SIDE :]
    total = refs.pop(0) if level else None
    outs = [refs.pop(0) for _ in range(2 if last else 1)]
    raw, ordered = refs.pop(0), refs.pop(0)
    new_total = refs.pop(0) if last else outs[0]
    sem = refs.pop(0)
    load_maps(level, own, got, where_ref, raw, ordered, sem)
    chunk = 2 * own[0].shape[2]
    blob = bundles[0].shape[0] // SIDE
    for t in range(new_total.shape[1] // TILE):
        columns = slice(t * TILE, (t + 1) * TILE)
        update = product(ordered, bundles, blob, chunk, t)
        new_total[:, columns] = update if total is None else total[:, columns] + update
    if last:
        split(where_ref[CHIPS], new_total, 3, outs)


def schur_step(level, last, where, own, got, bundles, state, arrow_t, after):
    arrow = arrow_t is not None
    rows, cols = state.shape
    depth = own.shape[3]
    blob = bundles[0].shape[0] // SIDE
    shape = jax.ShapeDtypeStruct
    if last:
        out_shape = [shape((rows // 2, cols), F32)] * 2
    else:
        out_shape = [shape((rows, cols), F32), shape((blob, TILE), BF16)]
    scratch = [pltpu.VMEM((rows, depth), BF16)] * 2
    if arrow:
        out_shape.append(shape(arrow_t.shape, F32))
        scratch.append(pltpu.VMEM((arrow_t.shape[0], depth), BF16))
    if last:
        scratch.append(pltpu.VMEM((rows, cols), F32))
    scratch.append(pltpu.SemaphoreType.DMA((2,)))
    late = [] if after is None else [after]
    operands = [where, own, got, *bundles, state] + ([arrow_t] if arrow else []) + late
    return pl.pallas_call(
        functools.partial(schur_kernel, level, last, arrow, len(late)),
        out_shape=out_shape,
        in_specs=[SMEM, ANY, ANY] + [VMEM] * (SIDE + (2 if arrow else 1)) + [ANY] * len(late),
        out_specs=[VMEM] * len(out_shape),
        scratch_shapes=scratch,
        compiler_params=params(),
        cost_estimate=cost(rows, depth, cols),
        name=f"schur_{level}",
    )(*operands)


def fill_step(level, last, where, maps, bundles, rows, cols, total, after):
    depth = maps[0].shape[3]
    shape = jax.ShapeDtypeStruct
    tall = 3 * rows
    if last:
        out_shape = [shape((tall // 2, cols), F32)] * 2
    else:
        out_shape = [shape((tall, cols), F32)]
    scratch = [pltpu.VMEM((tall, depth), BF16)] * 2
    if last:
        scratch.append(pltpu.VMEM((tall, cols), F32))
    scratch.append(pltpu.SemaphoreType.DMA((6,)))
    operands = [where, *maps, *bundles, after] + ([total] if level else [])
    return pl.pallas_call(
        functools.partial(fill_kernel, level, last),
        out_shape=out_shape,
        in_specs=[SMEM] + [ANY] * 6 + [VMEM] * SIDE + [ANY] + [VMEM] * (1 if level else 0),
        out_specs=[VMEM] * len(out_shape),
        scratch_shapes=scratch,
        compiler_params=params(),
        cost_estimate=cost(tall, depth, cols),
        name=f"fill_{level}",
    )(*operands)


def around(block, first):
    return [lax.ppermute(block, "panel", ring(first, step)) for step in (-1, 2, 1)]


def every_partition(tip, core, blocks):
    count = lax.axis_size("tm")
    half = count // 2
    width = lax.axis_size("panel")
    parts = [tip]
    for k in range(half):
        pairs = []
        for p in range(count):
            for i in range(width):
                away = k if i % 2 == 0 else half + k
                if away:
                    pairs.append((p * width + i, (p ^ away) * width + i))
        parts.append(lax.ppermute(tip, ("tm", "panel"), pairs))
    parts, blocks = lax.optimization_barrier((parts, blocks))
    parts = [jnp.where(core == 0, parts[0], parts[1]), *parts[2:]]
    while len(parts) > 1:
        parts = [parts[i] + parts[i + 1] for i in range(0, len(parts), 2)]
    return parts[0] + lax.ppermute(parts[0], "panel", SWAP), blocks


def shards(
    boundary,
    far_coupling,
    cross_coupling,
    tail_coupling,
    arrow_block,
    inverse_map,
    fill_map,
    cross_map,
    tail_map,
    arrow_tip,
    inverse_diagonal,
):
    levels = lax.axis_size("tm").bit_length() - 1
    rows, cols = boundary.shape[1:]
    chunk = 2 * rows
    count = SETS
    width = cols // 2 // count
    place = lax.axis_index("panel")
    core = place % 2
    y, x = place // 2 // SIDE, place // 2 % SIDE
    number = jnp.arange(CHIPS, dtype=jnp.int32)
    inner, outer = number % SIDE, number // SIDE
    up, across = jnp.where(core == 0, outer, inner), jnp.where(core == 0, inner, outer)
    order = ((y + up) % SIDE * SIDE + (x + across) % SIDE) * chunk
    where = jnp.concatenate([order, core[None]]).astype(jnp.int32)

    arrow = arrow_block[0]
    diagonal = inverse_diagonal[0]
    away = jnp.where(core == 0, boundary[0][:, cols // 2 :], boundary[0][:, : cols // 2])
    got = lax.ppermute(jnp.concatenate([away, arrow, diagonal[:, None]], axis=1), "panel", SWAP)
    got_half = got[:, : cols // 2]
    got_arrow = got[:, cols // 2 : cols // 2 + arrow.shape[1]]
    got_diagonal = got[:, -1]

    def paired(mine, theirs, axis):
        return jnp.where(
            core == 0, jnp.concatenate([mine, theirs], axis=axis), jnp.concatenate([theirs, mine], axis=axis)
        )

    arrow_t = paired(arrow.T, got_arrow.T, 1)
    weights = paired(diagonal, got_diagonal, 0)

    maps = (inverse_map, fill_map, cross_map, tail_map)
    got_maps = [lax.ppermute(m, "panel", SWAP) for m in maps]
    fill_maps = [*maps[1:], *got_maps[1:]]

    shape = jax.ShapeDtypeStruct
    extra = [arrow_t.shape[0] // 2] + [0] * (count - 1)
    begun = pl.pallas_call(
        start_kernel,
        out_shape=[shape((chunk, width), F32)] * count
        + [shape((chunk * (width // TILE) + more, TILE), BF16) for more in extra],
        in_specs=[SMEM, VMEM, VMEM, VMEM],
        out_specs=[VMEM] * (2 * count),
        compiler_params=params(),
        name="start",
    )(where, boundary[0], got_half, arrow_t)

    states, blobs, totals = list(begun[:count]), list(begun[count:]), [None] * count
    kept, sent = [None] * count, [None] * count
    def begin(blob, level, total):
        got = flip(blob, 1 << level)
        if total is not None:
            got, total = lax.optimization_barrier((got, total))
        return jnp.concatenate([got, *around(got, 0)], axis=0), total

    bundles = [None] * count
    for j in range(count):
        bundles[j], _ = begin(blobs[j], 0, None)
    for level in range(levels):
        last = level == levels - 1
        for j in range(count):
            pieces = [bundles[j], *around(bundles[j], 1)]
            other = None if (j == 0 and level == 0) else bundles[(j + 1) % count]
            if last:
                other = None
            result = schur_step(
                level, last, where, inverse_map, got_maps[0], pieces, states[j], arrow_t if j == 0 else None, other
            )
            if j == 0:
                arrow_t = result[2]
            filled = fill_step(level, last, where, fill_maps, pieces, chunk, width, totals[j], result[1])
            if last:
                kept[j] = jnp.concatenate([result[0], filled[0]], axis=0)
                sent[j] = jnp.concatenate([result[1], filled[1]], axis=0)
            else:
                states[j] = result[0]
                bundles[j], totals[j] = begin(result[1], level + 1, filled[0])

    tip = jnp.dot(arrow_t * weights[None, :], arrow_t.T, precision=lax.Precision.HIGHEST, preferred_element_type=F32)
    for axis in range(2):
        first, second, third = (lax.ppermute(tip, "panel", routes(axis, (k, k))) for k in (1, 2, 3))
        tip = (tip + first) + (second + third)
    back = [lax.ppermute(part, "panel", SWAP) for part in sent]
    tip, back[-1] = lax.optimization_barrier((tip, back[-1]))

    def whole(k):
        here = slice(k * rows, (k + 1) * rows)
        mine = [part[here] for part in kept]
        theirs = [part[here] for part in back]
        return jnp.where(core == 0, jnp.concatenate(mine + theirs, axis=1), jnp.concatenate(theirs + mine, axis=1))

    arrow_cols = jnp.where(core == 0, arrow_t[:, :rows], arrow_t[:, rows:]).T
    blocks = [
        whole(0),
        far_coupling[0] - whole(1),
        cross_coupling[0] - whole(2),
        tail_coupling[0] - whole(3),
        arrow_cols,
    ]
    tip, blocks = every_partition(tip, core, blocks)
    return (*(block[None] for block in blocks), arrow_tip - tip)


def solution(mesh):
    in_specs = (
        P("tm", "panel", None),
        P("tm", "panel", None),
        P("tm", "panel", None),
        P("tm", "panel", None),
        P("tm", "panel", None),
        P("tm", None, "panel", None),
        P("tm", None, "panel", None),
        P("tm", None, "panel", None),
        P("tm", None, "panel", None),
        P(),
        P("tm", "panel"),
    )
    out_specs = (
        P("tm", "panel", None),
        P("tm", "panel", None),
        P("tm", "panel", None),
        P("tm", "panel", None),
        P("tm", "panel", None),
        P(),
    )
    return jax.shard_map(shards, mesh=mesh, in_specs=in_specs, out_specs=out_specs, check_vma=False)
```

```python
import functools

import jax
import jax.numpy as jnp
from jax import lax
from jax.experimental import pallas as pl
from jax.experimental.pallas import tpu as pltpu
from jax.sharding import PartitionSpec as P

F32 = jnp.float32
BF16 = jnp.bfloat16
SETS = 2
SIDE = 4
CHIPS = SIDE * SIDE
TILE = 256
ANY = pl.BlockSpec(memory_space=pl.ANY)
VMEM = pl.BlockSpec(memory_space=pltpu.VMEM)
SMEM = pl.BlockSpec(memory_space=pltpu.SMEM)
NT = (((1,), (1,)), ((), ()))


def routes(axis, flips):
    out = []
    for y in range(SIDE):
        for x in range(SIDE):
            for core in range(2):
                to_y, to_x = (y, x ^ flips[core]) if axis == 0 else (y ^ flips[core], x)
                out.append(((y * SIDE + x) * 2 + core, (to_y * SIDE + to_x) * 2 + core))
    return out


def ring(first, step):
    out = []
    for y in range(SIDE):
        for x in range(SIDE):
            for core in range(2):
                to_y, to_x = (y, (x + step) % SIDE) if core == first else ((y + step) % SIDE, x)
                out.append(((y * SIDE + x) * 2 + core, (to_y * SIDE + to_x) * 2 + core))
    return out


SWAP = [(i, i ^ 1) for i in range(2 * CHIPS)]


def flip(block, bit):
    count = lax.axis_size("tm")
    return lax.ppermute(block, "tm", [(p, p ^ bit) for p in range(count)])


def params():
    return pltpu.CompilerParams(vmem_limit_bytes=24 * 1024 * 1024)


def cost(rows, depth, cols):
    return pl.CostEstimate(
        flops=2 * rows * depth * cols, bytes_accessed=2 * depth * (cols + rows) + 8 * rows * cols, transcendentals=0
    )


def pack(blob_ref, state, arrow_t):
    rows, cols = state.shape
    for t in range(cols // TILE):
        blob_ref[t * rows : (t + 1) * rows, :] = state[:, t * TILE : (t + 1) * TILE].astype(BF16)
    if arrow_t is not None:
        base = rows * (cols // TILE)
        half = arrow_t.shape[0] // 2
        blob_ref[base : base + half, :rows] = arrow_t[:half].astype(BF16)
        blob_ref[base : base + half, rows:] = arrow_t[half:].astype(BF16)


def start_kernel(where_ref, own_ref, got_ref, arrow_ref, *outs):
    core = where_ref[CHIPS]
    rows = own_ref.shape[0]
    count = len(outs) // 2
    width = outs[0].shape[1]
    mine = pl.ds(pl.multiple_of(core * rows, rows), rows)
    theirs = pl.ds(pl.multiple_of((1 - core) * rows, rows), rows)
    for j in range(count):
        state = outs[j]
        column = pl.multiple_of(core * count * width + j * width, width)
        state[mine, :] = own_ref[:, pl.ds(column, width)]
        state[theirs, :] = got_ref[:, j * width : (j + 1) * width]
        pack(outs[count + j], state[...], arrow_ref[...] if j == 0 else None)


def load_maps(level, own, got, where_ref, raw, ordered, sem):
    core = where_ref[CHIPS]
    rows = own[0].shape[2]
    copies = []
    for k in range(len(own)):
        for at, ref in ((core, own[k]), (1 - core, got[k])):
            at = pl.ds(pl.multiple_of((2 * k + at) * rows, rows), rows)
            copies.append(pltpu.make_async_copy(ref.at[0, level], raw.at[at], sem.at[len(copies)]))
    for copy in copies:
        copy.start()
    for copy in copies:
        copy.wait()
    chunk = 2 * rows
    for k in range(CHIPS):
        at = pl.multiple_of(where_ref[k], chunk)
        ordered[:, k * chunk : (k + 1) * chunk] = raw[:, pl.ds(at, chunk)]


def tile_of(bundle, blob, chunk, t):
    count = bundle.shape[0] // blob
    if blob == chunk:
        return bundle[...]
    return jnp.concatenate([bundle[k * blob + t * chunk : k * blob + (t + 1) * chunk, :] for k in range(count)], axis=0)


def product(ordered, bundles, blob, chunk, t):
    total = None
    start = 0
    for bundle in bundles:
        depth = bundle.shape[0] // blob * chunk
        term = jnp.dot(
            ordered[:, start : start + depth], tile_of(bundle, blob, chunk, t), preferred_element_type=F32
        )
        total = term if total is None else total + term
        start += depth
    return total


def schur_kernel(level, last, arrow, late, *refs):
    refs = list(refs)
    where_ref, own, got = refs[:3]
    bundles = refs[3 : 3 + SIDE]
    state = refs[3 + SIDE]
    refs = refs[4 + SIDE :]
    arrow_in = refs.pop(0) if arrow else None
    if late:
        refs.pop(0)
    outs = [refs.pop(0) for _ in range(2)]
    arrow_out = refs.pop(0) if arrow else None
    raw, ordered = refs.pop(0), refs.pop(0)
    arrow_buf = refs.pop(0) if arrow else None
    new_state = refs.pop(0) if last else outs[0]
    sem = refs.pop(0)
    load_maps(level, (own,), (got,), where_ref, raw, ordered, sem)
    chunk, cols = state.shape
    tiles = cols // TILE
    blob = bundles[0].shape[0] // SIDE
    new_arrow = None
    if arrow:
        half = arrow_in.shape[0] // 2
        for k in range(CHIPS):
            bundle, at = bundles[k // SIDE], k % SIDE * blob + tiles * chunk
            for h in range(2):
                arrow_buf[h * half : (h + 1) * half, k * chunk : (k + 1) * chunk] = bundle[
                    at : at + half, h * chunk : (h + 1) * chunk
                ]
        new_arrow = arrow_in[...] - lax.dot_general(arrow_buf[...], ordered[...], NT, preferred_element_type=F32)
        arrow_out[...] = new_arrow
    for t in range(tiles):
        columns = slice(t * TILE, (t + 1) * TILE)
        new_state[:, columns] = state[:, columns] - product(ordered, bundles, blob, chunk, t)
    if last:
        split(where_ref[CHIPS], new_state, 1, outs)
    else:
        pack(outs[1], new_state[...], new_arrow)


def split(core, total, count, outs):
    rows = total.shape[0] // count // 2
    keep, send = outs
    for k in range(count):
        here = slice(k * rows, (k + 1) * rows)
        keep[here, :] = total[pl.ds(pl.multiple_of((2 * k + core) * rows, rows), rows), :]
        send[here, :] = total[pl.ds(pl.multiple_of((2 * k + 1 - core) * rows, rows), rows), :]


def fill_kernel(level, last, *refs):
    refs = list(refs)
    where_ref = refs[0]
    own, got = refs[1:4], refs[4:7]
    bundles = refs[7 : 7 + SIDE]
    refs = refs[8 + SIDE :]
    total = refs.pop(0) if level else None
    outs = [refs.pop(0) for _ in range(2 if last else 1)]
    raw, ordered = refs.pop(0), refs.pop(0)
    new_total = refs.pop(0) if last else outs[0]
    sem = refs.pop(0)
    load_maps(level, own, got, where_ref, raw, ordered, sem)
    chunk = 2 * own[0].shape[2]
    blob = bundles[0].shape[0] // SIDE
    for t in range(new_total.shape[1] // TILE):
        columns = slice(t * TILE, (t + 1) * TILE)
        update = product(ordered, bundles, blob, chunk, t)
        new_total[:, columns] = update if total is None else total[:, columns] + update
    if last:
        split(where_ref[CHIPS], new_total, 3, outs)


def schur_step(level, last, where, own, got, bundles, state, arrow_t, after):
    arrow = arrow_t is not None
    rows, cols = state.shape
    depth = own.shape[3]
    blob = bundles[0].shape[0] // SIDE
    shape = jax.ShapeDtypeStruct
    if last:
        out_shape = [shape((rows // 2, cols), F32)] * 2
    else:
        out_shape = [shape((rows, cols), F32), shape((blob, TILE), BF16)]
    scratch = [pltpu.VMEM((rows, depth), BF16)] * 2
    if arrow:
        out_shape.append(shape(arrow_t.shape, F32))
        scratch.append(pltpu.VMEM((arrow_t.shape[0], depth), BF16))
    if last:
        scratch.append(pltpu.VMEM((rows, cols), F32))
    scratch.append(pltpu.SemaphoreType.DMA((2,)))
    late = [] if after is None else [after]
    operands = [where, own, got, *bundles, state] + ([arrow_t] if arrow else []) + late
    return pl.pallas_call(
        functools.partial(schur_kernel, level, last, arrow, len(late)),
        out_shape=out_shape,
        in_specs=[SMEM, ANY, ANY] + [VMEM] * (SIDE + (2 if arrow else 1)) + [ANY] * len(late),
        out_specs=[VMEM] * len(out_shape),
        scratch_shapes=scratch,
        compiler_params=params(),
        cost_estimate=cost(rows, depth, cols),
        name=f"schur_{level}",
    )(*operands)


def fill_step(level, last, where, maps, bundles, rows, cols, total, after):
    depth = maps[0].shape[3]
    shape = jax.ShapeDtypeStruct
    tall = 3 * rows
    if last:
        out_shape = [shape((tall // 2, cols), F32)] * 2
    else:
        out_shape = [shape((tall, cols), F32)]
    scratch = [pltpu.VMEM((tall, depth), BF16)] * 2
    if last:
        scratch.append(pltpu.VMEM((tall, cols), F32))
    scratch.append(pltpu.SemaphoreType.DMA((6,)))
    operands = [where, *maps, *bundles, after] + ([total] if level else [])
    return pl.pallas_call(
        functools.partial(fill_kernel, level, last),
        out_shape=out_shape,
        in_specs=[SMEM] + [ANY] * 6 + [VMEM] * SIDE + [ANY] + [VMEM] * (1 if level else 0),
        out_specs=[VMEM] * len(out_shape),
        scratch_shapes=scratch,
        compiler_params=params(),
        cost_estimate=cost(tall, depth, cols),
        name=f"fill_{level}",
    )(*operands)


def around(block, first):
    return [lax.ppermute(block, "panel", ring(first, step)) for step in (-1, 2, 1)]


def every_partition(tip, core, blocks):
    count = lax.axis_size("tm")
    half = count // 2
    width = lax.axis_size("panel")
    parts = [tip]
    for k in range(half):
        pairs = []
        for p in range(count):
            for i in range(width):
                away = k if i % 2 == 0 else half + k
                if away:
                    pairs.append((p * width + i, (p ^ away) * width + i))
        parts.append(lax.ppermute(tip, ("tm", "panel"), pairs))
    parts, blocks = lax.optimization_barrier((parts, blocks))
    parts = [jnp.where(core == 0, parts[0], parts[1]), *parts[2:]]
    while len(parts) > 1:
        parts = [parts[i] + parts[i + 1] for i in range(0, len(parts), 2)]
    return parts[0] + lax.ppermute(parts[0], "panel", SWAP), blocks


def shards(
    boundary,
    far_coupling,
    cross_coupling,
    tail_coupling,
    arrow_block,
    inverse_map,
    fill_map,
    cross_map,
    tail_map,
    arrow_tip,
    inverse_diagonal,
):
    levels = lax.axis_size("tm").bit_length() - 1
    rows, cols = boundary.shape[1:]
    chunk = 2 * rows
    count = SETS
    width = cols // 2 // count
    place = lax.axis_index("panel")
    core = place % 2
    y, x = place // 2 // SIDE, place // 2 % SIDE
    number = jnp.arange(CHIPS, dtype=jnp.int32)
    inner, outer = number % SIDE, number // SIDE
    up, across = jnp.where(core == 0, outer, inner), jnp.where(core == 0, inner, outer)
    order = ((y + up) % SIDE * SIDE + (x + across) % SIDE) * chunk
    where = jnp.concatenate([order, core[None]]).astype(jnp.int32)

    arrow = arrow_block[0]
    diagonal = inverse_diagonal[0]
    away = jnp.where(core == 0, boundary[0][:, cols // 2 :], boundary[0][:, : cols // 2])
    got = lax.ppermute(jnp.concatenate([away, arrow, diagonal[:, None]], axis=1), "panel", SWAP)
    got_half = got[:, : cols // 2]
    got_arrow = got[:, cols // 2 : cols // 2 + arrow.shape[1]]
    got_diagonal = got[:, -1]

    def paired(mine, theirs, axis):
        return jnp.where(
            core == 0, jnp.concatenate([mine, theirs], axis=axis), jnp.concatenate([theirs, mine], axis=axis)
        )

    arrow_t = paired(arrow.T, got_arrow.T, 1)
    weights = paired(diagonal, got_diagonal, 0)

    maps = (inverse_map, fill_map, cross_map, tail_map)
    got_maps = [lax.ppermute(m, "panel", SWAP) for m in maps]
    fill_maps = [*maps[1:], *got_maps[1:]]

    shape = jax.ShapeDtypeStruct
    extra = [arrow_t.shape[0] // 2] + [0] * (count - 1)
    begun = pl.pallas_call(
        start_kernel,
        out_shape=[shape((chunk, width), F32)] * count
        + [shape((chunk * (width // TILE) + more, TILE), BF16) for more in extra],
        in_specs=[SMEM, VMEM, VMEM, VMEM],
        out_specs=[VMEM] * (2 * count),
        compiler_params=params(),
        name="start",
    )(where, boundary[0], got_half, arrow_t)

    states, blobs, totals = list(begun[:count]), list(begun[count:]), [None] * count
    kept, sent = [None] * count, [None] * count
    def begin(blob, level, total):
        got = flip(blob, 1 << level)
        if total is not None:
            got, total = lax.optimization_barrier((got, total))
        return jnp.concatenate([got, *around(got, 0)], axis=0), total

    bundles = [None] * count
    for j in range(count):
        bundles[j], _ = begin(blobs[j], 0, None)
    for level in range(levels):
        last = level == levels - 1
        for j in range(count):
            pieces = [bundles[j], *around(bundles[j], 1)]
            other = None if (j == 0 and level == 0) else bundles[(j + 1) % count]
            if last and j == count - 1:
                other = None
            result = schur_step(
                level, last, where, inverse_map, got_maps[0], pieces, states[j], arrow_t if j == 0 else None, other
            )
            if j == 0:
                arrow_t = result[2]
            filled = fill_step(level, last, where, fill_maps, pieces, chunk, width, totals[j], result[1])
            if last:
                kept[j] = jnp.concatenate([result[0], filled[0]], axis=0)
                sent[j] = jnp.concatenate([result[1], filled[1]], axis=0)
            else:
                states[j] = result[0]
                bundles[j], totals[j] = begin(result[1], level + 1, filled[0])

    tip = jnp.dot(arrow_t * weights[None, :], arrow_t.T, precision=lax.Precision.HIGHEST, preferred_element_type=F32)
    for axis in range(2):
        for k in (1, 3):
            tip = tip + lax.ppermute(tip, "panel", routes(axis, (k, k)))

    back = [lax.ppermute(part, "panel", SWAP) for part in sent]
    tip, back[-1] = lax.optimization_barrier((tip, back[-1]))

    def whole(k):
        here = slice(k * rows, (k + 1) * rows)
        mine = [part[here] for part in kept]
        theirs = [part[here] for part in back]
        return jnp.where(core == 0, jnp.concatenate(mine + theirs, axis=1), jnp.concatenate(theirs + mine, axis=1))

    arrow_cols = jnp.where(core == 0, arrow_t[:, :rows], arrow_t[:, rows:]).T
    blocks = [
        whole(0),
        far_coupling[0] - whole(1),
        cross_coupling[0] - whole(2),
        tail_coupling[0] - whole(3),
        arrow_cols,
    ]
    tip, blocks = every_partition(tip, core, blocks)
    return (*(block[None] for block in blocks), arrow_tip - tip)


def solution(mesh):
    in_specs = (
        P("tm", "panel", None),
        P("tm", "panel", None),
        P("tm", "panel", None),
        P("tm", "panel", None),
        P("tm", "panel", None),
        P("tm", None, "panel", None),
        P("tm", None, "panel", None),
        P("tm", None, "panel", None),
        P("tm", None, "panel", None),
        P(),
        P("tm", "panel"),
    )
    out_specs = (
        P("tm", "panel", None),
        P("tm", "panel", None),
        P("tm", "panel", None),
        P("tm", "panel", None),
        P("tm", "panel", None),
        P(),
    )
    return jax.shard_map(shards, mesh=mesh, in_specs=in_specs, out_specs=out_specs, check_vma=False)
```
